512 devices in a mesh: rep: 8 (over z), gx: 4 (over y_hi), gy: 4 (over y_lo, core), gz: 4 (over x).
Axes of the slice: x: 4, y: 8 (y_hi: 4, y_lo: 2; y = y_hi * 2 + y_lo), z: 8, core: 2. Of those that a mesh axis runs over, the one named last changes fastest.
Arguments:
- context: bfloat16 [16384, 6144], P(('rep', 'gx'), ('gy', 'gz')), may hold values from -6 to 6
- out_grad: bfloat16 [16384, 6144], P(('rep', 'gy', 'gz'), 'gx'), may hold values from -6 to 6
- kept_values: bfloat16 [3072, 6144], P(('gy', 'gz'), 'gx'), may hold values from -0.109375 to 0.109375
- keep_codes: int32 [1536, 6144], P(('gy', 'gz'), 'gx'), may hold values from 0 to 5
Outputs:
- context_grad: bfloat16 [16384, 6144], P(('rep', 'gx'), ('gy', 'gz'))
- kept_grad: bfloat16 [3072, 6144], P(('gy', 'gz'), 'gx')
The draws below stay inside these ranges and needn't reach their ends.
Inputs may be any that keep to these rules, and one draw needn't show every extreme that they name: `keep_codes`: code 0 keeps positions (0, 1), 1 keeps (0, 2), 2 keeps (0, 3), 3 keeps (1, 2), 4 keeps (1, 3), 5 keeps (2, 3) of its group of four input rows.
All inputs are finite; a program needn't handle non-finite values.
Results may differ from the reference program's by a relative error of at most 0.001.
Values may be sent and summed in bfloat16 or wider, within the bound.
A program may use at most 64 MiB of HBM per device.

```python
import jax
import jax.numpy as jnp
from jax import lax

DIN = 6144
DOUT = 6144
TOKENS = 16384


def set_ends(entries, key, least, top_value):
    longest = entries.shape.index(max(entries.shape))
    spots = []
    for shift in (0, 1):
        where = [jax.random.randint(jax.random.fold_in(key, axis), (), 0, length) for axis, length in enumerate(entries.shape)]
        where[longest] = (where[longest] + shift) % entries.shape[longest]
        spots.append(tuple(where))
    return entries.at[spots[0]].set(least).at[spots[1]].set(top_value)


def shard_levels(own_key, extent, cuts, low, largest):
    def one(axis_at, blocks):
        draws = jax.random.uniform(jax.random.fold_in(jax.random.fold_in(own_key, 6), axis_at), (blocks,), jnp.float32, low / len(cuts), largest / len(cuts))
        return jnp.repeat(jnp.exp(draws), extent[axis_at] // blocks).reshape((-1,) + (1,) * (len(extent) - axis_at - 1))

    level = one(*cuts[0])
    for cut in cuts[1:]:
        level = level * one(*cut)
    return level


def gaussian(key, dims, spread, reach, cuts=(), kind=jnp.bfloat16):
    factor_of = shard_levels(key, dims, cuts, -0.22, 0.18) if cuts else 1.0
    drawn = jax.random.normal(key, dims, jnp.float32) * spread * factor_of
    return jnp.minimum(jnp.maximum(drawn, -reach), reach).astype(kind)


def setup_inputs(seed: int = 0) -> dict:
    key_list = jax.random.split(jax.random.key(seed), 5)
    return {
        "context": gaussian(key_list[0], (TOKENS, DIN), 1.0, 6.0, ((0, 32), (1, 16))),
        "out_grad": gaussian(key_list[1], (TOKENS, DOUT), 1.0, 6.0, ((0, 128), (1, 4))),
        "kept_values": gaussian(key_list[2], (DIN // 2, DOUT), (DOUT // 2) ** -0.5, 0.109375, ((0, 16), (1, 4))),
        "keep_codes": set_ends(jax.random.randint(key_list[3], (DIN // 4, DOUT), 0, 6), jax.random.fold_in(key_list[3], 1), 0, 5).astype(jnp.int32),
    }


def kept_positions(codes):
    lower_pos = jnp.where(codes < 3, 0, jnp.where(codes < 5, 1, 2)).astype(jnp.int32)
    upper_pos = jnp.where(codes == 0, 1, jnp.where((codes == 1) | (codes == 3), 2, 3)).astype(jnp.int32)
    return lower_pos, upper_pos


def expand_pairs(values, codes):
    groups, columns = codes.shape
    lower_pos, upper_pos = kept_positions(codes)
    paired = values.reshape(groups, 2, columns)
    slot_ids = jnp.arange(4, dtype=jnp.int32)[None, :, None]
    zero_value = jnp.zeros((), values.dtype)
    dense = jnp.where(slot_ids == lower_pos[:, None, :], paired[:, 0:1, :],
                      jnp.where(slot_ids == upper_pos[:, None, :], paired[:, 1:2, :], zero_value))
    return dense.reshape(4 * groups, columns)


def compress_pairs(dense, codes):
    groups, columns = codes.shape
    lower_pos, upper_pos = kept_positions(codes)
    blocks = dense.reshape(groups, 4, columns)
    slot_ids = jnp.arange(4, dtype=jnp.int32)[None, :, None]
    zero_value = jnp.zeros((), dense.dtype)
    first_kept = jnp.sum(jnp.where(slot_ids == lower_pos[:, None, :], blocks, zero_value), axis=1)
    second_kept = jnp.sum(jnp.where(slot_ids == upper_pos[:, None, :], blocks, zero_value), axis=1)
    return jnp.stack([first_kept, second_kept], axis=1).reshape(2 * groups, columns)


def reference(context, out_grad, kept_values, keep_codes):
    dense_weight = expand_pairs(kept_values, keep_codes)
    context_grad = lax.dot_general(out_grad, dense_weight, (((1,), (1,)), ((), ())),
                                   preferred_element_type=jnp.float32).astype(jnp.bfloat16)
    full_grad = lax.dot_general(context, out_grad, (((0,), (0,)), ((), ())),
                                preferred_element_type=jnp.float32)
    full_grad = full_grad * (TOKENS ** -0.5)
    kept_grad = compress_pairs(full_grad, keep_codes).astype(jnp.bfloat16)
    return context_grad, kept_grad
```

```python
import jax
import jax.numpy as jnp
from jax import lax
from jax.experimental import pallas as pl
from jax.experimental.pallas import tpu as pltpu
from jax.sharding import PartitionSpec as P

MESH = pl.DeviceIdType.MESH
BF = jnp.bfloat16
F32 = jnp.float32

def dot_nn(a, b):
    return lax.dot_general(a, b, (((1,), (0,)), ((), ())), preferred_element_type=F32)

def dot_nt(a, b):
    return lax.dot_general(a, b, (((1,), (1,)), ((), ())), preferred_element_type=F32)

def one_hot(rows, cols, hit):
    r = lax.broadcasted_iota(jnp.int32, (rows, cols), 0)
    c = lax.broadcasted_iota(jnp.int32, (rows, cols), 1)
    return jnp.where(hit(r, c), 1.0, 0.0).astype(BF)

def kernel(
    ctx_hbm, grad_hbm, kept_hbm, codes_hbm, cg_ref, kg_ref,
    gb, cb, cpt, ws, kept_v, codes_v, rs_out, rs_in, ag, acc,
    load_sem, gs, gr, ts, tr, cs, cr, wys, wyr, wzs, wzr, rss, rsr, ags, agr,
):
    z = lax.axis_index("rep")
    q = lax.axis_index("gx")
    p = lax.axis_index("gy")
    x = lax.axis_index("gz")
    core = p % 2
    twin_p = (p + 2) % 4
    core_p = p + 1 - 2 * core
    core_twin_p = (core_p + 2) % 4
    xr, xl = (x + 1) % 4, (x + 3) % 4
    qr, ql, qo = (q + 1) % 4, (q + 3) % 4, (q + 2) % 4
    up = 1 - 2 * core

    at_twin = (z, q, twin_p, x)
    at_core = (z, q, core_p, x)
    at_xr = (z, q, p, xr)
    at_xl = (z, q, p, xl)
    at_qr = (z, qr, p, x)
    at_ql = (z, ql, p, x)
    at_flip = (z, p, q, x)

    def at_z(step):
        return ((z + step + 8) % 8, q, p, x)

    sends = []

    def copy(src, dst, ssem, rsem, device):
        return pltpu.make_async_remote_copy(
            src_ref=src, dst_ref=dst, send_sem=ssem, recv_sem=rsem,
            device_id=device, device_id_type=MESH,
        )

    loads = []
    for k in range(4):
        loads.append(pltpu.make_async_copy(
            grad_hbm.at[:, pl.ds(k * 384, 384)], gb.at[0, k, p, x], load_sem.at[k]))
    for j in range(3):
        loads.append(pltpu.make_async_copy(
            ctx_hbm.at[:, pl.ds(j * 128, 128)], cb.at[q, j], load_sem.at[4 + j]))
    loads.append(pltpu.make_async_copy(kept_hbm, kept_v, load_sem.at[7]))
    loads.append(pltpu.make_async_copy(codes_hbm, codes_v, load_sem.at[8]))
    for ld in loads:
        ld.start()

    barrier = pltpu.get_barrier_semaphore()
    for device in [at_twin, at_core, at_xr, at_xl, at_qr, at_ql] + [at_z(s) for s in range(1, 8)]:
        pl.semaphore_signal(barrier, inc=1, device_id=device, device_id_type=MESH)

    @pl.when(p != q)
    def _():
        pl.semaphore_signal(barrier, inc=1, device_id=at_flip, device_id_type=MESH)

    for ld in loads:
        ld.wait()
    split = one_hot(192, 192, lambda r, c: c == 2 * (r % 96) + r // 96)
    for k in range(4):
        cols = pl.ds(k * 384, 384)
        both = dot_nn(split, kept_v[:, cols]).astype(BF)
        numbers = codes_v[:, cols].astype(F32).astype(BF)
        ws[q, k] = both[:144]
        ws[q, 4 + k, 0:48] = both[144:]
        ws[q, 4 + k, 48:144] = numbers

    pl.semaphore_wait(barrier, jnp.where(p != q, 14, 13))

    def guarded(ph, block_p, run):
        if ph == 0:
            run()
        else:
            pl.when(block_p != q)(run)

    def g_copy(ph, k, block, si, ri, device):
        ref = gb.at[ph, k, block[0], block[1]]
        return copy(ref, ref, gs.at[ph * 4 + k, si], gr.at[ph * 4 + k, ri], device)

    def g_send(ph, k, block, si, ri, device):
        guarded(ph, block[0], lambda: g_copy(ph, k, block, si, ri, device).start())
        sends.append(lambda: guarded(
            ph, block[0], lambda: g_copy(ph, k, block, si, ri, device).wait_send()))

    def g_wait(ph, k, block, ri):
        guarded(ph, block[0], lambda: g_copy(ph, k, block, 0, ri, at_core).wait_recv())

    def g_row(ph, k, block_p, si, ri):
        ref = gb.at[ph, k, block_p]
        return copy(ref, ref, gs.at[ph * 4 + k, si], gr.at[ph * 4 + k, ri], at_core)

    def g_core(ph, k, block_p, si, ri):
        guarded(ph, block_p, lambda: g_row(ph, k, block_p, si, ri).start())
        sends.append(lambda: guarded(
            ph, block_p, lambda: g_row(ph, k, block_p, si, ri).wait_send()))

    def g_core_wait(ph, k):
        guarded(ph, core_p, lambda: g_row(ph, k, core_p, 7, 7).wait_recv())
        guarded(ph, core_twin_p, lambda: g_row(ph, k, core_twin_p, 8, 8).wait_recv())

    def g_twin_send(ph, k):
        g_send(ph, k, (p, x), 0, 0, at_twin)

    def g_own(ph, k):
        g_send(ph, k, (p, x), 1, 1, at_xr)
        g_send(ph, k, (p, x), 2, 2, at_xl)

    def g_twin(ph, k):
        g_wait(ph, k, (twin_p, x), 0)
        g_send(ph, k, (twin_p, x), 3, 3, at_xr)
        g_send(ph, k, (twin_p, x), 4, 4, at_xl)

    def g_forward(ph, k):
        g_wait(ph, k, (p, xl), 1)
        g_send(ph, k, (p, xl), 5, 5, at_xr)
        g_wait(ph, k, (twin_p, xr), 4)
        g_send(ph, k, (twin_p, xr), 6, 6, at_xl)

    def g_last(ph, k):
        g_wait(ph, k, (p, xr), 2)
        g_wait(ph, k, (twin_p, xl), 3)
        g_wait(ph, k, (p, (x + 2) % 4), 5)
        g_core(ph, k, p, 7, 7)
        g_wait(ph, k, (twin_p, (x + 2) % 4), 6)
        g_core(ph, k, twin_p, 8, 8)

    def t_copy(k):
        return copy(gb.at[0, k, p, x], gb.at[1, k, q, x], ts.at[k], tr.at[k], at_flip)

    def t_send(k):
        pl.when(p != q)(lambda: t_copy(k).start())
        sends.append(lambda: pl.when(p != q)(lambda: t_copy(k).wait_send()))

    def t_wait(k):
        pl.when(p != q)(lambda: copy(
            gb.at[1, k, p, x], gb.at[1, k, p, x], ts.at[k], tr.at[k], at_flip).wait_recv())

    def c_copy(j, block_q, ri, device):
        if ri < 2:
            ref = cb.at[block_q, j]
        else:
            ref = cb.at[block_q, j, pl.ds((ri - 2) * 256, 256)]
        return copy(ref, ref, cs.at[j, ri], cr.at[j, ri], device)

    def c_send(j, block_q, ri, device):
        c_copy(j, block_q, ri, device).start()
        sends.append(lambda: c_copy(j, block_q, ri, device).wait_send())

    def c_own(j):
        c_send(j, q, 0, at_qr)
        c_send(j, q, 1, at_ql)

    def c_forward(j):
        c_copy(j, ql, 0, at_qr).wait_recv()
        c_send(j, ql, 2, at_qr)
        c_copy(j, qr, 1, at_qr).wait_recv()
        c_send(j, qr, 3, at_ql)

    def c_last(j):
        c_copy(j, qo, 2, at_qr).wait_recv()
        c_copy(j, qo, 3, at_qr).wait_recv()

    def wy_copy(block_q, ri, device):
        ref = ws.at[block_q, z]
        return copy(ref, ref, wys.at[ri], wyr.at[ri], device)

    def wy_own():
        for ri, device in ((0, at_qr), (1, at_ql)):
            wy_copy(q, ri, device).start()
            sends.append(lambda ri=ri, device=device: wy_copy(q, ri, device).wait_send())

    def wy_forward():
        wy_copy(ql, 0, at_qr).wait_recv()
        pl.when(core == 0)(lambda: wy_copy(ql, 2, at_qr).start())
        wy_copy(qr, 1, at_qr).wait_recv()
        pl.when(core == 1)(lambda: wy_copy(qr, 2, at_ql).start())
        sends.append(lambda: wy_copy(ql, 2, at_qr).wait_send())

    def wz_copy(m, block_q, slice_z, ri, device):
        ref = ws.at[block_q, slice_z]
        return copy(ref, ref, wzs.at[m, ri], wzr.at[m, ri], device)

    def wz_send(m, step):
        block_q = (ql, qr, qo)[m]
        todo = []
        if step <= 4:
            todo.append(((z - (step - 1) * up + 8) % 8, step - 1, at_z(up)))
        if step <= 3:
            todo.append(((z + (step - 1) * up + 8) % 8, 3 + step, at_z(-up)))
        for slice_z, ri, device in todo:
            wz_copy(m, block_q, slice_z, ri, device).start()
            sends.append(lambda a=(m, block_q, slice_z, ri, device): wz_copy(*a).wait_send())

    def wz_wait(m, step):
        block_q = (ql, qr, qo)[m]
        wz_copy(m, block_q, (z - step * up + 8) % 8, step - 1, at_core).wait_recv()
        if step <= 3:
            wz_copy(m, block_q, (z + step * up + 8) % 8, 3 + step, at_core).wait_recv()

    def kg_part(j):
        turn = one_hot(128, 128, lambda r, c: c == 4 * (r % 32) + r // 32)
        for b in range(4):
            cpt[:, b * 512:(b + 1) * 512] = dot_nt(turn, cb[b, j]).astype(BF)

        for k in range(4):
            cols = pl.ds(k * 384, 384)
            dense = dot_nn(cpt[...], gb[0, k].reshape(2048, 384))
            codes = codes_v[32 * j:32 * j + 32, cols]
            d0, d1, d2, d3 = (dense[32 * s:32 * s + 32] for s in range(4))
            first = jnp.where(codes < 3, d0, jnp.where(codes < 5, d1, d2))
            second = jnp.where(
                codes == 0, d1, jnp.where((codes == 1) | (codes == 3), d2, d3))
            for s in range(4):
                rs_out[j, s, :, cols] = first[8 * s:8 * s + 8]
                rs_out[j, 4 + s, :, cols] = second[8 * s:8 * s + 8]

    def rs_copy(j, step):
        return copy(rs_out.at[j, (z + step) % 8], rs_in.at[j, step - 1],
                    rss.at[j, step - 1], rsr.at[j, step - 1], at_z(step))

    def rs_send(j):
        for step in (4, 3, 5, 2, 6, 1, 7):
            rs_copy(j, step).start()
            sends.append(lambda step=step: rs_copy(j, step).wait_send())

    def ag_copy(j, step, slice_z):
        ref = ag.at[j, slice_z]
        return copy(ref, ref, ags.at[j, step - 1], agr.at[j, step - 1], at_z(step))

    def rs_finish(j):
        for step in range(1, 8):
            rs_copy(j, step).wait_recv()
        total = rs_out[j, z]
        for step in range(7):
            total = total + rs_in[j, step]
        total = total * (16384.0 ** -0.5)
        ag[j, z] = jnp.concatenate([total[:, :768], total[:, 768:]], 0).astype(BF)
        for step in (4, 3, 5, 2, 6, 1, 7):
            ag_copy(j, step, z).start()
            sends.append(lambda step=step: ag_copy(j, step, z).wait_send())

    def ag_wait(j):
        for step in range(1, 8):
            ag_copy(j, step, (z - step + 8) % 8).wait_recv()

    def kg_store():
        rows = ag[...].reshape(384, 768)
        for h in range(2):
            def hit(r, c, h=h):
                slot, group = r % 2, r // 2
                want = (((group // 32) * 8 + slot * 4 + (group % 32) // 8) * 2 + h) * 8 + group % 8
                return c == want

            kg_ref[:, h * 768:(h + 1) * 768] = dot_nn(one_hot(192, 384, hit), rows).astype(BF)

    def weights(block_q, k):
        top, low = ws[block_q, k], ws[block_q, 4 + k]
        k0 = top[:96].astype(F32)
        k1 = jnp.concatenate([top[96:], low[:48]], 0).astype(F32)
        code = low[48:].astype(F32)
        w0 = jnp.where(code < 2.5, k0, 0.0)
        w1 = jnp.where(code < 0.5, k1, jnp.where((code > 2.5) & (code < 4.5), k0, 0.0))
        is2 = ((code > 0.5) & (code < 1.5)) | ((code > 2.5) & (code < 3.5))
        w2 = jnp.where(code > 4.5, k0, jnp.where(is2, k1, 0.0))
        is3 = ((code > 1.5) & (code < 2.5)) | (code > 3.5)
        w3 = jnp.where(is3, k1, 0.0)
        return jnp.concatenate([w0, w1, w2, w3], 0).astype(BF)

    def cg_own():
        total = jnp.zeros((512, 384), F32)
        for k in range(4):
            total = total + dot_nt(gb[0, k, q].reshape(512, 384), weights(q, k))
        acc[...] = total

    def cg_add(k):
        for b in (ql, qr, qo):
            acc[...] += dot_nt(gb[1, k, b].reshape(512, 384), weights(b, k))

    def cg_store():
        back = one_hot(384, 384, lambda r, c: c == 4 * (r % 96) + r // 96)
        cg_ref[...] = dot_nn(acc[...].astype(BF), back).astype(BF)

    for k in range(4):
        g_twin_send(0, k)
        g_own(0, k)
    wy_own()
    c_own(0)
    g_twin(0, 0)
    wy_forward()
    wz_send(0, 1)
    wz_send(1, 1)
    g_forward(0, 0)
    c_own(1)
    g_twin(0, 1)
    wy_copy(qo, 2, at_qr).wait_recv()
    wz_send(2, 1)
    c_forward(0)
    g_forward(0, 1)
    g_last(0, 0)
    c_own(2)
    g_twin(0, 2)
    for m in range(3):
        wz_wait(m, 1)
        wz_send(m, 2)
    g_forward(0, 2)
    g_last(0, 1)
    for k in range(4):
        t_send(k)
    g_twin(0, 3)
    c_last(0)
    c_forward(1)
    for m in range(3):
        wz_wait(m, 2)
        wz_send(m, 3)
    g_forward(0, 3)
    g_last(0, 2)
    c_forward(2)
    g_last(0, 3)
    for m in range(3):
        wz_wait(m, 3)
        wz_send(m, 4)
    for k in range(4):
        g_core_wait(0, k)
    c_last(1)
    for k in range(4):
        t_wait(k)
        g_twin_send(1, k)
        g_own(1, k)
    kg_part(0)
    rs_send(0)
    g_twin(1, 0)
    g_forward(1, 0)
    kg_part(1)
    rs_send(1)
    g_twin(1, 1)
    g_forward(1, 1)
    g_last(1, 0)
    c_last(2)
    kg_part(2)
    rs_send(2)
    g_twin(1, 2)
    g_forward(1, 2)
    g_last(1, 1)
    rs_finish(0)
    cg_own()
    g_twin(1, 3)
    g_forward(1, 3)
    g_last(1, 2)
    for m in range(3):
        wz_wait(m, 4)
    rs_finish(1)
    g_core_wait(1, 0)
    cg_add(0)
    g_last(1, 3)
    g_core_wait(1, 1)
    cg_add(1)
    rs_finish(2)
    g_core_wait(1, 2)
    cg_add(2)
    g_core_wait(1, 3)
    cg_add(3)
    cg_store()
    for j in range(3):
        ag_wait(j)
    kg_store()
    for wait in sends:
        wait()

def local(context, out_grad, kept_values, keep_codes):
    dma = pltpu.SemaphoreType.DMA
    return pl.pallas_call(
        kernel,
        out_shape=(
            jax.ShapeDtypeStruct((512, 384), BF),
            jax.ShapeDtypeStruct((192, 1536), BF),
        ),
        in_specs=[pl.BlockSpec(memory_space=pl.ANY)] * 4,
        out_specs=(pl.BlockSpec(memory_space=pltpu.VMEM),) * 2,
        scratch_shapes=[
            pltpu.VMEM((2, 4, 4, 4, 128, 384), BF),
            pltpu.VMEM((4, 3, 512, 128), BF),
            pltpu.VMEM((128, 2048), BF),
            pltpu.VMEM((4, 8, 144, 384), BF),
            pltpu.VMEM((192, 1536), BF),
            pltpu.VMEM((96, 1536), jnp.int32),
            pltpu.VMEM((3, 8, 8, 1536), F32),
            pltpu.VMEM((3, 7, 8, 1536), F32),
            pltpu.VMEM((3, 8, 16, 768), BF),
            pltpu.VMEM((512, 384), F32),
            dma((9,)),

            dma((8, 9)),
            dma((8, 9)),
            dma((4,)),
            dma((4,)),
            dma((3, 4)),
            dma((3, 4)),
            dma((3,)),
            dma((3,)),
            dma((3, 7)),
            dma((3, 7)),
            dma((3, 7)),
            dma((3, 7)),
            dma((3, 7)),
            dma((3, 7)),
        ],
        compiler_params=pltpu.CompilerParams(
            collective_id=0, has_side_effects=True, vmem_limit_bytes=56 << 20
        ),
        cost_estimate=pl.CostEstimate(
            flops=4 * 2048 * 384 * 1536, bytes_accessed=3 << 20, transcendentals=0
        ),
        name="sparse_backward",
    )(context, out_grad, kept_values, keep_codes)

def solution(mesh):
    in_specs = (
        P(("rep", "gx"), ("gy", "gz")),
        P(("rep", "gy", "gz"), "gx"),
        P(("gy", "gz"), "gx"),
        P(("gy", "gz"), "gx"),
    )
    out_specs = (P(("rep", "gx"), ("gy", "gz")), P(("gy", "gz"), "gx"))
    return jax.shard_map(local, mesh=mesh, in_specs=in_specs, out_specs=out_specs, check_vma=False)
```

```python
import jax
import jax.numpy as jnp
from jax import lax
from jax.experimental import pallas as pl
from jax.experimental.pallas import tpu as pltpu
from jax.sharding import PartitionSpec as P

MESH = pl.DeviceIdType.MESH
BF = jnp.bfloat16
F32 = jnp.float32

def dot_nn(a, b):
    return lax.dot_general(a, b, (((1,), (0,)), ((), ())), preferred_element_type=F32)

def dot_nt(a, b):
    return lax.dot_general(a, b, (((1,), (1,)), ((), ())), preferred_element_type=F32)

def one_hot(rows, cols, hit):
    r = lax.broadcasted_iota(jnp.int32, (rows, cols), 0)
    c = lax.broadcasted_iota(jnp.int32, (rows, cols), 1)
    return jnp.where(hit(r, c), 1.0, 0.0).astype(BF)

def kernel(
    ctx_hbm, grad_hbm, kept_hbm, codes_hbm, cg_ref, kg_ref,
    gb, cb, cpt, ws, kept_v, codes_v, rs_out, rs_in, ag, acc,
    load_sem, gs, gr, ts, tr, cs, cr, wys, wyr, wzs, wzr, rss, rsr, ags, agr,
):
    z = lax.axis_index("rep")
    q = lax.axis_index("gx")
    p = lax.axis_index("gy")
    x = lax.axis_index("gz")
    core = p % 2
    twin_p = (p + 2) % 4
    core_p = p + 1 - 2 * core
    core_twin_p = (core_p + 2) % 4
    xr, xl = (x + 1) % 4, (x + 3) % 4
    qr, ql, qo = (q + 1) % 4, (q + 3) % 4, (q + 2) % 4
    up = 1 - 2 * core

    at_twin = (z, q, twin_p, x)
    at_core = (z, q, core_p, x)
    at_xr = (z, q, p, xr)
    at_xl = (z, q, p, xl)
    at_qr = (z, qr, p, x)
    at_ql = (z, ql, p, x)
    delta = (p - q + 4) % 4
    t_slots = ((delta * delta - delta) // 2, (delta // 2) * delta)
    at_source = (z, (q + 3 - (p + 1) // 2) % 4, q, x)

    def at_z(step):
        return ((z + step + 8) % 8, q, p, x)

    sends = []

    def copy(src, dst, ssem, rsem, device):
        return pltpu.make_async_remote_copy(
            src_ref=src, dst_ref=dst, send_sem=ssem, recv_sem=rsem,
            device_id=device, device_id_type=MESH,
        )

    loads = []
    for k in range(4):
        loads.append(pltpu.make_async_copy(
            grad_hbm.at[:, pl.ds(k * 384, 384)], gb.at[0, k, p, x], load_sem.at[k]))
    for j in range(3):
        loads.append(pltpu.make_async_copy(
            ctx_hbm.at[:, pl.ds(j * 128, 128)], cb.at[q, j], load_sem.at[4 + j]))
    loads.append(pltpu.make_async_copy(kept_hbm, kept_v, load_sem.at[7]))
    loads.append(pltpu.make_async_copy(codes_hbm, codes_v, load_sem.at[8]))
    for ld in loads:
        ld.start()

    barrier = pltpu.get_barrier_semaphore()
    for device in [at_twin, at_core, at_xr, at_xl, at_qr, at_ql] + [at_z(s) for s in range(1, 8)]:
        pl.semaphore_signal(barrier, inc=1, device_id=device, device_id_type=MESH)

    pl.semaphore_signal(barrier, inc=1, device_id=at_source, device_id_type=MESH)

    @pl.when(delta != 0)
    def _():
        pl.semaphore_signal(
            barrier, inc=1, device_id=(z, p, t_slots[0], x), device_id_type=MESH)

    @pl.when(delta == 2)
    def _():
        pl.semaphore_signal(
            barrier, inc=1, device_id=(z, p, t_slots[1], x), device_id_type=MESH)

    for ld in loads:
        ld.wait()
    split = one_hot(192, 192, lambda r, c: c == 2 * (r % 96) + r // 96)
    for k in range(4):
        cols = pl.ds(k * 384, 384)
        both = dot_nn(split, kept_v[:, cols]).astype(BF)
        numbers = codes_v[:, cols].astype(F32).astype(BF)
        ws[q, k] = both[:144]
        ws[q, 4 + k, 0:48] = both[144:]
        ws[q, 4 + k, 48:144] = numbers

    pl.semaphore_wait(barrier, jnp.where(delta == 0, 14, jnp.where(delta == 2, 16, 15)))

    def guarded(ph, k, block_p, run):
        if ph == 0:
            run()
        else:
            pl.when(block_p != (2 if k < 2 else 1))(run)

    def g_copy(ph, k, block, si, ri, device):
        ref = gb.at[ph, k, block[0], block[1]]
        return copy(ref, ref, gs.at[ph * 4 + k, si], gr.at[ph * 4 + k, ri], device)

    def g_send(ph, k, block, si, ri, device):
        guarded(ph, k, block[0], lambda: g_copy(ph, k, block, si, ri, device).start())
        sends.append(lambda: guarded(
            ph, k, block[0], lambda: g_copy(ph, k, block, si, ri, device).wait_send()))

    def g_wait(ph, k, block, ri):
        guarded(ph, k, block[0], lambda: g_copy(ph, k, block, 0, ri, at_core).wait_recv())

    def g_row(ph, k, block_p, si, ri):
        ref = gb.at[ph, k, block_p]
        return copy(ref, ref, gs.at[ph * 4 + k, si], gr.at[ph * 4 + k, ri], at_core)

    def g_core(ph, k, block_p, si, ri):
        guarded(ph, k, block_p, lambda: g_row(ph, k, block_p, si, ri).start())
        sends.append(lambda: guarded(
            ph, k, block_p, lambda: g_row(ph, k, block_p, si, ri).wait_send()))

    def g_core_wait(ph, k):
        guarded(ph, k, core_p, lambda: g_row(ph, k, core_p, 7, 7).wait_recv())
        guarded(ph, k, core_twin_p, lambda: g_row(ph, k, core_twin_p, 8, 8).wait_recv())

    def g_twin_send(ph, k):
        g_send(ph, k, (p, x), 0, 0, at_twin)

    def g_own(ph, k):
        g_send(ph, k, (p, x), 1, 1, at_xr)
        g_send(ph, k, (p, x), 2, 2, at_xl)

    def g_twin(ph, k):
        g_wait(ph, k, (twin_p, x), 0)
        g_send(ph, k, (twin_p, x), 3, 3, at_xr)
        g_send(ph, k, (twin_p, x), 4, 4, at_xl)

    def g_fwd_own(ph, k):
        g_wait(ph, k, (p, xl), 1)
        g_send(ph, k, (p, xl), 5, 5, at_xr)

    def g_fwd_twin(ph, k):
        g_wait(ph, k, (twin_p, xr), 4)
        g_send(ph, k, (twin_p, xr), 6, 6, at_xl)

    def g_core_own(ph, k):
        g_wait(ph, k, (p, xr), 2)
        g_wait(ph, k, (p, (x + 2) % 4), 5)
        g_core(ph, k, p, 7, 7)

    def g_core_twin(ph, k):
        g_wait(ph, k, (twin_p, xl), 3)
        g_wait(ph, k, (twin_p, (x + 2) % 4), 6)
        g_core(ph, k, twin_p, 8, 8)

    def t_copy(k):
        slot = t_slots[k // 2]
        return copy(gb.at[0, k, p, x], gb.at[1, k, slot, x], ts.at[k], tr.at[k], (z, p, slot, x))

    def t_send(k):
        pl.when(delta != 0)(lambda: t_copy(k).start())
        sends.append(lambda: pl.when(delta != 0)(lambda: t_copy(k).wait_send()))

    def t_wait(k):
        ref = gb.at[1, k, p, x]
        guarded(1, k, p, lambda: copy(ref, ref, ts.at[k], tr.at[k], at_core).wait_recv())

    def c_copy(j, block_q, ri, device):
        if ri < 2:
            ref = cb.at[block_q, j]
        else:
            ref = cb.at[block_q, j, pl.ds((ri - 2) * 256, 256)]
        return copy(ref, ref, cs.at[j, ri], cr.at[j, ri], device)

    def c_send(j, block_q, ri, device):
        c_copy(j, block_q, ri, device).start()
        sends.append(lambda: c_copy(j, block_q, ri, device).wait_send())

    def c_own(j):
        c_send(j, q, 0, at_qr)
        c_send(j, q, 1, at_ql)

    def c_fwd(way, j):
        if way == 0:
            c_copy(j, ql, 0, at_qr).wait_recv()
            c_send(j, ql, 2, at_qr)
        else:
            c_copy(j, qr, 1, at_qr).wait_recv()
            c_send(j, qr, 3, at_ql)

    def c_last(j):
        c_copy(j, qo, 2, at_qr).wait_recv()
        c_copy(j, qo, 3, at_qr).wait_recv()

    def wy_copy(block_q, ri, device):
        ref = ws.at[block_q, z]
        return copy(ref, ref, wys.at[ri], wyr.at[ri], device)

    def wy_own():
        for ri, device in ((0, at_qr), (1, at_ql)):
            wy_copy(q, ri, device).start()
            sends.append(lambda ri=ri, device=device: wy_copy(q, ri, device).wait_send())

    def wy_fwd(way):
        if way == 0:
            wy_copy(ql, 0, at_qr).wait_recv()
            pl.when(core == 0)(lambda: wy_copy(ql, 2, at_qr).start())
        else:
            wy_copy(qr, 1, at_qr).wait_recv()
            pl.when(core == 1)(lambda: wy_copy(qr, 2, at_ql).start())
            sends.append(lambda: wy_copy(ql, 2, at_qr).wait_send())

    def wz_copy(m, block_q, slice_z, ri, device):
        ref = ws.at[block_q, slice_z]
        return copy(ref, ref, wzs.at[m, ri], wzr.at[m, ri], device)

    def wz_send(m, step):
        block_q = (ql, qr, qo)[m]
        todo = []
        if step <= 4:
            todo.append(((z - (step - 1) * up + 8) % 8, step - 1, at_z(up)))
        if step <= 3:
            todo.append(((z + (step - 1) * up + 8) % 8, 3 + step, at_z(-up)))
        for slice_z, ri, device in todo:
            wz_copy(m, block_q, slice_z, ri, device).start()
            sends.append(lambda a=(m, block_q, slice_z, ri, device): wz_copy(*a).wait_send())

    def wz_wait(m, step):
        block_q = (ql, qr, qo)[m]
        wz_copy(m, block_q, (z - step * up + 8) % 8, step - 1, at_core).wait_recv()
        if step <= 3:
            wz_copy(m, block_q, (z + step * up + 8) % 8, 3 + step, at_core).wait_recv()

    def wz_step(m, step):
        if step > 1:
            wz_wait(m, step - 1)
        elif m == 2:
            wy_copy(qo, 2, at_qr).wait_recv()
        wz_send(m, step)

    def kg_part(j):
        if j == 0:
            for k in range(4):
                g_core_wait(0, k)
        c_last(j)
        turn = one_hot(128, 128, lambda r, c: c == 4 * (r % 32) + r // 32)
        for b in range(4):
            cpt[:, b * 512:(b + 1) * 512] = dot_nt(turn, cb[b, j]).astype(BF)

        for k in range(4):
            cols = pl.ds(k * 384, 384)
            dense = dot_nn(cpt[...], gb[0, k].reshape(2048, 384))
            codes = codes_v[32 * j:32 * j + 32, cols]
            d0, d1, d2, d3 = (dense[32 * s:32 * s + 32] for s in range(4))
            first = jnp.where(codes < 3, d0, jnp.where(codes < 5, d1, d2))
            second = jnp.where(
                codes == 0, d1, jnp.where((codes == 1) | (codes == 3), d2, d3))
            for s in range(4):
                rs_out[j, s, :, cols] = first[8 * s:8 * s + 8]
                rs_out[j, 4 + s, :, cols] = second[8 * s:8 * s + 8]
        rs_send(j, 1)

    def rs_copy(j, step, way):
        if way == 0:
            ref, slot, device = rs_out.at[j, (z + (5 - step) * up + 8) % 8], step - 1, at_z(up)
        else:
            ref, slot, device = rs_out.at[j, (z - (4 - step) * up + 8) % 8], 3 + step, at_z(-up)
        return copy(ref, rs_in.at[j, slot], rss.at[j, slot], rsr.at[j, slot], device)

    def rs_send(j, step):
        for way in range(2 if step < 4 else 1):
            rs_copy(j, step, way).start()
            sends.append(lambda way=way: rs_copy(j, step, way).wait_send())

    def rs_step(j, step):
        rs_copy(j, step, 0).wait_recv()
        rs_out[j, (z + (4 - step) * up + 8) % 8] += rs_in[j, step - 1]
        rs_copy(j, step, 1).wait_recv()
        rs_out[j, (z - (3 - step) * up + 8) % 8] += rs_in[j, 3 + step]
        rs_send(j, step + 1)

    def ag_copy(j, step, slice_z):
        ref = ag.at[j, slice_z]
        return copy(ref, ref, ags.at[j, step - 1], agr.at[j, step - 1], at_z(step))

    def rs_finish(j):
        rs_copy(j, 4, 0).wait_recv()
        total = (rs_out[j, z] + rs_in[j, 3]) * (16384.0 ** -0.5)
        ag[j, z] = jnp.concatenate([total[:, :768], total[:, 768:]], 0).astype(BF)
        for step in (4, 3, 5, 2, 6, 1, 7):
            ag_copy(j, step, z).start()
            sends.append(lambda step=step: ag_copy(j, step, z).wait_send())

    def ag_wait(j):
        for step in range(1, 8):
            ag_copy(j, step, (z - step + 8) % 8).wait_recv()

    def kg_store():
        for j in range(3):
            ag_wait(j)
        rows = ag[...].reshape(384, 768)
        for h in range(2):
            def hit(r, c, h=h):
                slot, group = r % 2, r // 2
                want = (((group // 32) * 8 + slot * 4 + (group % 32) // 8) * 2 + h) * 8 + group % 8
                return c == want

            kg_ref[:, h * 768:(h + 1) * 768] = dot_nn(one_hot(192, 384, hit), rows).astype(BF)

    def weights(block_q, k):
        top, low = ws[block_q, k], ws[block_q, 4 + k]
        k0 = top[:96].astype(F32)
        k1 = jnp.concatenate([top[96:], low[:48]], 0).astype(F32)
        code = low[48:].astype(F32)
        w0 = jnp.where(code < 2.5, k0, 0.0)
        w1 = jnp.where(code < 0.5, k1, jnp.where((code > 2.5) & (code < 4.5), k0, 0.0))
        is2 = ((code > 0.5) & (code < 1.5)) | ((code > 2.5) & (code < 3.5))
        w2 = jnp.where(code > 4.5, k0, jnp.where(is2, k1, 0.0))
        is3 = ((code > 1.5) & (code < 2.5)) | (code > 3.5)
        w3 = jnp.where(is3, k1, 0.0)
        return jnp.concatenate([w0, w1, w2, w3], 0).astype(BF)

    def cg_own():
        total = jnp.zeros((512, 384), F32)
        for k in range(4):
            total = total + dot_nt(gb[0, k, q].reshape(512, 384), weights(q, k))
        acc[...] = total

    def cg_add(k):
        if k == 0:
            for m in range(3):
                wz_wait(m, 4)
        g_core_wait(1, k)
        for slot, b in ((0, ql), (3, qr), (1 if k < 2 else 2, qo)):
            acc[...] += dot_nt(gb[1, k, slot].reshape(512, 384), weights(b, k))

    def cg_store():
        back = one_hot(384, 384, lambda r, c: c == 4 * (r % 96) + r // 96)
        cg_ref[...] = dot_nn(acc[...].astype(BF), back).astype(BF)

    g_twin_send(0, 0)
    g_own(0, 0)
    g_twin_send(0, 1)
    g_own(0, 1)
    g_twin_send(0, 2)
    g_twin_send(0, 3)
    wy_own()
    g_own(0, 2)
    g_fwd_own(0, 0)
    g_own(0, 3)
    g_fwd_own(0, 1)
    c_own(0)
    g_twin(0, 0)
    g_fwd_own(0, 2)
    g_twin(0, 1)
    g_core_own(0, 0)
    g_fwd_own(0, 3)
    g_core_own(0, 1)
    g_twin(0, 2)
    g_twin(0, 3)
    wy_fwd(0)
    wy_fwd(1)
    wz_step(0, 1)
    wz_step(1, 1)
    c_own(1)
    g_fwd_twin(0, 0)
    c_fwd(0, 0)
    c_fwd(1, 0)
    g_fwd_twin(0, 1)
    wz_step(0, 2)
    wz_step(1, 2)
    g_fwd_twin(0, 2)
    g_fwd_twin(0, 3)
    c_own(2)
    g_core_twin(0, 0)
    g_core_own(0, 2)
    g_core_own(0, 3)
    wz_step(2, 1)
    g_core_twin(0, 1)
    wz_step(0, 3)
    wz_step(1, 3)
    g_core_twin(0, 2)
    g_core_twin(0, 3)
    c_fwd(0, 1)
    c_fwd(1, 1)
    t_send(0)
    t_send(2)
    wz_step(2, 2)
    kg_part(0)
    cg_own()
    c_fwd(0, 2)
    c_fwd(1, 2)
    t_send(1)
    wz_step(0, 4)
    wz_step(1, 4)
    kg_part(1)
    rs_step(0, 1)
    wz_step(2, 3)
    t_wait(0)
    g_twin_send(1, 0)
    g_own(1, 0)
    t_wait(2)
    g_twin_send(1, 2)
    g_own(1, 2)
    kg_part(2)
    t_wait(1)
    g_twin_send(1, 1)
    g_own(1, 1)
    t_send(3)
    rs_step(1, 1)
    rs_step(0, 2)
    wz_step(2, 4)
    g_fwd_own(1, 0)
    rs_step(2, 1)
    g_twin(1, 0)
    g_fwd_own(1, 2)
    g_twin(1, 2)
    g_fwd_own(1, 1)
    rs_step(1, 2)
    rs_step(0, 3)
    g_twin(1, 1)
    t_wait(3)
    g_twin_send(1, 3)
    g_own(1, 3)
    rs_step(2, 2)
    g_fwd_twin(1, 0)
    rs_step(1, 3)
    rs_finish(0)
    g_core_own(1, 0)
    g_fwd_twin(1, 2)
    rs_step(2, 3)
    g_twin(1, 3)
    g_fwd_twin(1, 1)
    rs_finish(1)
    g_core_own(1, 2)
    g_core_twin(1, 0)
    g_core_own(1, 1)
    g_fwd_own(1, 3)
    g_core_twin(1, 2)
    cg_add(0)
    g_fwd_twin(1, 3)
    g_core_twin(1, 1)
    rs_finish(2)
    cg_add(2)
    cg_add(1)
    g_core_own(1, 3)
    g_core_twin(1, 3)
    cg_add(3)
    kg_store()
    cg_store()
    for wait in sends:
        wait()


def local(context, out_grad, kept_values, keep_codes):
    dma = pltpu.SemaphoreType.DMA
    return pl.pallas_call(
        kernel,
        out_shape=(
            jax.ShapeDtypeStruct((512, 384), BF),
            jax.ShapeDtypeStruct((192, 1536), BF),
        ),
        in_specs=[pl.BlockSpec(memory_space=pl.ANY)] * 4,
        out_specs=(pl.BlockSpec(memory_space=pltpu.VMEM),) * 2,
        scratch_shapes=[
            pltpu.VMEM((2, 4, 4, 4, 128, 384), BF),
            pltpu.VMEM((4, 3, 512, 128), BF),
            pltpu.VMEM((128, 2048), BF),
            pltpu.VMEM((4, 8, 144, 384), BF),
            pltpu.VMEM((192, 1536), BF),
            pltpu.VMEM((96, 1536), jnp.int32),
            pltpu.VMEM((3, 8, 8, 1536), F32),
            pltpu.VMEM((3, 7, 8, 1536), F32),
            pltpu.VMEM((3, 8, 16, 768), BF),
            pltpu.VMEM((512, 384), F32),
            dma((9,)),

            dma((8, 9)),
            dma((8, 9)),
            dma((4,)),
            dma((4,)),
            dma((3, 4)),
            dma((3, 4)),
            dma((3,)),
            dma((3,)),
            dma((3, 7)),
            dma((3, 7)),
            dma((3, 7)),
            dma((3, 7)),
            dma((3, 7)),
            dma((3, 7)),
        ],
        compiler_params=pltpu.CompilerParams(
            collective_id=0, has_side_effects=True, vmem_limit_bytes=56 << 20
        ),
        cost_estimate=pl.CostEstimate(
            flops=4 * 2048 * 384 * 1536, bytes_accessed=3 << 20, transcendentals=0
        ),
        name="sparse_backward",
    )(context, out_grad, kept_values, keep_codes)

def solution(mesh):
    in_specs = (
        P(("rep", "gx"), ("gy", "gz")),
        P(("rep", "gy", "gz"), "gx"),
        P(("gy", "gz"), "gx"),
        P(("gy", "gz"), "gx"),
    )
    out_specs = (P(("rep", "gx"), ("gy", "gz")), P(("gy", "gz"), "gx"))
    return jax.shard_map(local, mesh=mesh, in_specs=in_specs, out_specs=out_specs, check_vma=False)
```

```python
import jax
import jax.numpy as jnp
from jax import lax
from jax.experimental import pallas as pl
from jax.experimental.pallas import tpu as pltpu
from jax.sharding import PartitionSpec as P

MESH = pl.DeviceIdType.MESH
BF = jnp.bfloat16
F32 = jnp.float32

def dot_nn(a, b):
    return lax.dot_general(a, b, (((1,), (0,)), ((), ())), preferred_element_type=F32)

def dot_nt(a, b):
    return lax.dot_general(a, b, (((1,), (1,)), ((), ())), preferred_element_type=F32)

def one_hot(rows, cols, hit):
    r = lax.broadcasted_iota(jnp.int32, (rows, cols), 0)
    c = lax.broadcasted_iota(jnp.int32, (rows, cols), 1)
    return jnp.where(hit(r, c), 1.0, 0.0).astype(BF)

def kernel(
    ctx_hbm, grad_hbm, kept_hbm, codes_hbm, cg_ref, kg_ref,
    gb, cb, cpt, ws, kept_v, codes_v, rs_out, rs_in, ag, acc, wd,
    load_sem, gs, gr, ts, tr, cs, cr, wys, wyr, wzs, wzr, rss, rsr, ags, agr,
):
    z = lax.axis_index("rep")
    q = lax.axis_index("gx")
    p = lax.axis_index("gy")
    x = lax.axis_index("gz")
    core = p % 2
    twin_p = (p + 2) % 4
    core_p = p + 1 - 2 * core
    core_twin_p = (core_p + 2) % 4
    xr, xl = (x + 1) % 4, (x + 3) % 4
    qr, ql, qo = (q + 1) % 4, (q + 3) % 4, (q + 2) % 4
    up = 1 - 2 * core

    at_twin = (z, q, twin_p, x)
    at_core = (z, q, core_p, x)
    at_xr = (z, q, p, xr)
    at_xl = (z, q, p, xl)
    at_qr = (z, qr, p, x)
    at_ql = (z, ql, p, x)
    delta = (p - q + 4) % 4
    t_slots = ((delta * delta - delta) // 2, (delta // 2) * delta)
    at_source = (z, (q + 3 - (p + 1) // 2) % 4, q, x)

    def at_z(step):
        return ((z + step + 8) % 8, q, p, x)

    sends = []

    def copy(src, dst, ssem, rsem, device):
        return pltpu.make_async_remote_copy(
            src_ref=src, dst_ref=dst, send_sem=ssem, recv_sem=rsem,
            device_id=device, device_id_type=MESH,
        )

    loads = []
    for k in range(4):
        loads.append(pltpu.make_async_copy(
            grad_hbm.at[:, pl.ds(k * 384, 384)], gb.at[0, k, p, x], load_sem.at[k]))
    for j in range(3):
        loads.append(pltpu.make_async_copy(
            ctx_hbm.at[:, pl.ds(j * 128, 128)], cb.at[q, j], load_sem.at[4 + j]))
    loads.append(pltpu.make_async_copy(kept_hbm, kept_v, load_sem.at[7]))
    loads.append(pltpu.make_async_copy(codes_hbm, codes_v, load_sem.at[8]))
    for ld in loads:
        ld.start()

    barrier = pltpu.get_barrier_semaphore()
    for device in [at_twin, at_core, at_xr, at_xl, at_qr, at_ql] + [at_z(s) for s in range(1, 8)]:
        pl.semaphore_signal(barrier, inc=1, device_id=device, device_id_type=MESH)

    pl.semaphore_signal(barrier, inc=1, device_id=at_source, device_id_type=MESH)

    @pl.when(delta != 0)
    def _():
        pl.semaphore_signal(
            barrier, inc=1, device_id=(z, p, t_slots[0], x), device_id_type=MESH)

    @pl.when(delta == 2)
    def _():
        pl.semaphore_signal(
            barrier, inc=1, device_id=(z, p, t_slots[1], x), device_id_type=MESH)

    for ld in loads[:4]:
        ld.wait()
    pl.semaphore_wait(barrier, jnp.where(delta == 0, 14, jnp.where(delta == 2, 16, 15)))

    def prep():
        loads[7].wait()
        loads[8].wait()
        split = one_hot(192, 192, lambda r, c: c == 2 * (r % 96) + r // 96)
        for k in range(4):
            cols = pl.ds(k * 384, 384)
            both = dot_nn(split, kept_v[:, cols]).astype(BF)
            numbers = codes_v[:, cols].astype(F32).astype(BF)
            ws[q, k] = both[:144]
            ws[q, 4 + k, 0:48] = both[144:]
            ws[q, 4 + k, 48:144] = numbers

    def guarded(ph, k, block_p, run):
        if ph == 0:
            run()
        else:
            pl.when(block_p != (2 if k < 4 else 1))(run)

    def g_copy(ph, k, block, si, ri, device):
        ref = gb.at[ph, k // 2, block[0], block[1], pl.ds(k % 2 * 64, 64)]
        return copy(ref, ref, gs.at[ph * 8 + k, si], gr.at[ph * 8 + k, ri], device)

    def g_send(ph, k, block, si, ri, device):
        guarded(ph, k, block[0], lambda: g_copy(ph, k, block, si, ri, device).start())
        sends.append(lambda: guarded(
            ph, k, block[0], lambda: g_copy(ph, k, block, si, ri, device).wait_send()))

    def g_wait(ph, k, block, ri):
        guarded(ph, k, block[0], lambda: g_copy(ph, k, block, 0, ri, at_core).wait_recv())

    def g_row(ph, k, block_p, si, ri):
        ref = gb.at[ph, k // 2, block_p, pl.ds(0, 4), pl.ds(k % 2 * 64, 64)]
        return copy(ref, ref, gs.at[ph * 8 + k, si], gr.at[ph * 8 + k, ri], at_core)

    def g_core(ph, k, block_p, si, ri):
        guarded(ph, k, block_p, lambda: g_row(ph, k, block_p, si, ri).start())
        sends.append(lambda: guarded(
            ph, k, block_p, lambda: g_row(ph, k, block_p, si, ri).wait_send()))

    def g_core_wait(ph, k):
        guarded(ph, k, core_p, lambda: g_row(ph, k, core_p, 7, 7).wait_recv())
        guarded(ph, k, core_twin_p, lambda: g_row(ph, k, core_twin_p, 8, 8).wait_recv())

    def g_twin_send(ph, k):
        g_send(ph, k, (p, x), 0, 0, at_twin)

    def g_own(ph, k):
        g_send(ph, k, (p, x), 1, 1, at_xr)
        g_send(ph, k, (p, x), 2, 2, at_xl)

    def g_twin(ph, k):
        g_wait(ph, k, (twin_p, x), 0)
        g_send(ph, k, (twin_p, x), 3, 3, at_xr)
        g_send(ph, k, (twin_p, x), 4, 4, at_xl)

    def g_fwd_own(ph, k):
        g_wait(ph, k, (p, xl), 1)
        g_send(ph, k, (p, xl), 5, 5, at_xr)

    def g_fwd_twin(ph, k):
        g_wait(ph, k, (twin_p, xr), 4)
        g_send(ph, k, (twin_p, xr), 6, 6, at_xl)

    def g_core_own(ph, k):
        g_wait(ph, k, (p, xr), 2)
        g_wait(ph, k, (p, (x + 2) % 4), 5)
        g_core(ph, k, p, 7, 7)

    def g_core_twin(ph, k):
        g_wait(ph, k, (twin_p, xl), 3)
        g_wait(ph, k, (twin_p, (x + 2) % 4), 6)
        g_core(ph, k, twin_p, 8, 8)

    def t_copy(k):
        slot, rows = t_slots[k // 4], pl.ds(k % 2 * 64, 64)
        return copy(gb.at[0, k // 2, p, x, rows], gb.at[1, k // 2, slot, x, rows],
                    ts.at[k], tr.at[k], (z, p, slot, x))

    def t_send(k):
        pl.when(delta != 0)(lambda: t_copy(k).start())
        sends.append(lambda: pl.when(delta != 0)(lambda: t_copy(k).wait_send()))

    def t_wait(k):
        ref = gb.at[1, k // 2, p, x, pl.ds(k % 2 * 64, 64)]
        guarded(1, k, p, lambda: copy(ref, ref, ts.at[k], tr.at[k], at_core).wait_recv())

    def c_copy(j, block_q, ri, device):
        ref = cb.at[block_q, j, pl.ds((0, 256, 0, 256, 256, 0)[ri], 256)]
        return copy(ref, ref, cs.at[j, ri], cr.at[j, ri], device)

    def c_send(j, block_q, ri, device):
        c_copy(j, block_q, ri, device).start()
        sends.append(lambda: c_copy(j, block_q, ri, device).wait_send())

    def c_own(j):
        loads[4 + j].wait()
        c_send(j, q, 0, at_qr)
        c_send(j, q, 1, at_ql)
        c_send(j, q, 4, at_qr)
        c_send(j, q, 5, at_ql)

    def c_fwd(way, j):
        if way == 0:
            c_copy(j, ql, 0, at_qr).wait_recv()
            c_send(j, ql, 2, at_qr)
        else:
            c_copy(j, qr, 1, at_qr).wait_recv()
            c_send(j, qr, 3, at_ql)

    def c_last(j):
        for ri, block_q in ((4, ql), (5, qr), (2, qo), (3, qo)):
            c_copy(j, block_q, ri, at_qr).wait_recv()

    def wy_copy(block_q, ri, device):
        ref = ws.at[block_q, z]
        return copy(ref, ref, wys.at[ri], wyr.at[ri], device)

    def wy_own():
        for ri, device in ((0, at_qr), (1, at_ql)):
            wy_copy(q, ri, device).start()
            sends.append(lambda ri=ri, device=device: wy_copy(q, ri, device).wait_send())

    def wy_fwd(way):
        if way == 0:
            wy_copy(ql, 0, at_qr).wait_recv()
            pl.when(core == 0)(lambda: wy_copy(ql, 2, at_qr).start())
        else:
            wy_copy(qr, 1, at_qr).wait_recv()
            pl.when(core == 1)(lambda: wy_copy(qr, 2, at_ql).start())
            sends.append(lambda: wy_copy(ql, 2, at_qr).wait_send())

    def wz_copy(m, block_q, slice_z, ri, device):
        ref = ws.at[block_q, slice_z]
        return copy(ref, ref, wzs.at[m, ri], wzr.at[m, ri], device)

    def wz_send(m, step):
        block_q = (ql, qr, qo)[m]
        todo = []
        if step <= 4:
            todo.append(((z - (step - 1) * up + 8) % 8, step - 1, at_z(up)))
        if step <= 3:
            todo.append(((z + (step - 1) * up + 8) % 8, 3 + step, at_z(-up)))
        for slice_z, ri, device in todo:
            wz_copy(m, block_q, slice_z, ri, device).start()
            sends.append(lambda a=(m, block_q, slice_z, ri, device): wz_copy(*a).wait_send())

    def wz_wait(m, step):
        block_q = (ql, qr, qo)[m]
        wz_copy(m, block_q, (z - step * up + 8) % 8, step - 1, at_core).wait_recv()
        if step <= 3:
            wz_copy(m, block_q, (z + step * up + 8) % 8, 3 + step, at_core).wait_recv()

    def wz_step(m, step):
        if step > 1:
            wz_wait(m, step - 1)
        elif m == 2:
            wy_copy(qo, 2, at_qr).wait_recv()
        wz_send(m, step)

    def kg_part(j):
        c_last(j)
        turn = one_hot(128, 128, lambda r, c: c == 4 * (r % 32) + r // 32)
        for b in range(4):
            cpt[:, b * 512:(b + 1) * 512] = dot_nt(turn, cb[b, j]).astype(BF)

        for k in range(4):
            cols = pl.ds(k * 384, 384)
            dense = dot_nn(cpt[...], gb[0, k].reshape(2048, 384))
            codes = codes_v[32 * j:32 * j + 32, cols]
            d0, d1, d2, d3 = (dense[32 * s:32 * s + 32] for s in range(4))
            first = jnp.where(codes < 3, d0, jnp.where(codes < 5, d1, d2))
            second = jnp.where(
                codes == 0, d1, jnp.where((codes == 1) | (codes == 3), d2, d3))
            for s in range(4):
                rs_out[j, s, :, cols] = first[8 * s:8 * s + 8]
                rs_out[j, 4 + s, :, cols] = second[8 * s:8 * s + 8]
        rs_send(j, 1)

    def rs_copy(j, step, way):
        if way == 0:
            ref, slot, device = rs_out.at[j, (z + (5 - step) * up + 8) % 8], step - 1, at_z(up)
        else:
            ref, slot, device = rs_out.at[j, (z - (4 - step) * up + 8) % 8], 3 + step, at_z(-up)
        return copy(ref, rs_in.at[j, slot], rss.at[j, slot], rsr.at[j, slot], device)

    def rs_send(j, step):
        for way in range(2 if step < 4 else 1):
            rs_copy(j, step, way).start()
            sends.append(lambda way=way: rs_copy(j, step, way).wait_send())

    def rs_step(j, step):
        rs_copy(j, step, 0).wait_recv()
        rs_out[j, (z + (4 - step) * up + 8) % 8] += rs_in[j, step - 1]
        rs_copy(j, step, 1).wait_recv()
        rs_out[j, (z - (3 - step) * up + 8) % 8] += rs_in[j, 3 + step]
        rs_send(j, step + 1)

    def ag_copy(j, step, slice_z):
        ref = ag.at[j, slice_z]
        return copy(ref, ref, ags.at[j, step - 1], agr.at[j, step - 1], at_z(step))

    def rs_finish(j):
        rs_copy(j, 4, 0).wait_recv()
        total = (rs_out[j, z] + rs_in[j, 3]) * (16384.0 ** -0.5)
        ag[j, z] = jnp.concatenate([total[:, :768], total[:, 768:]], 0).astype(BF)
        for step in (4, 3, 5, 2, 6, 1, 7):
            ag_copy(j, step, z).start()
            sends.append(lambda step=step: ag_copy(j, step, z).wait_send())

    def ag_wait(j):
        for step in range(1, 8):
            ag_copy(j, step, (z - step + 8) % 8).wait_recv()

    def kg_store():
        for j in range(3):
            ag_wait(j)
        rows = ag[...].reshape(384, 768)
        for h in range(2):
            def hit(r, c, h=h):
                slot, group = r % 2, r // 2
                want = (((group // 32) * 8 + slot * 4 + (group % 32) // 8) * 2 + h) * 8 + group % 8
                return c == want

            kg_ref[:, h * 768:(h + 1) * 768] = dot_nn(one_hot(192, 384, hit), rows).astype(BF)

    def weights(block_q, k):
        top, low = ws[block_q, k], ws[block_q, 4 + k]
        k0 = top[:96].astype(F32)
        k1 = jnp.concatenate([top[96:], low[:48]], 0).astype(F32)
        code = low[48:].astype(F32)
        w0 = jnp.where(code < 2.5, k0, 0.0)
        w1 = jnp.where(code < 0.5, k1, jnp.where((code > 2.5) & (code < 4.5), k0, 0.0))
        is2 = ((code > 0.5) & (code < 1.5)) | ((code > 2.5) & (code < 3.5))
        w2 = jnp.where(code > 4.5, k0, jnp.where(is2, k1, 0.0))
        is3 = ((code > 1.5) & (code < 2.5)) | (code > 3.5)
        w3 = jnp.where(is3, k1, 0.0)
        return jnp.concatenate([w0, w1, w2, w3], 0).astype(BF)

    def cg_own():
        for k in range(8):
            g_core_wait(0, k)
        total = jnp.zeros((512, 384), F32)
        for k in range(4):
            total = total + dot_nt(gb[0, k, q].reshape(512, 384), weights(q, k))
        acc[...] = total.reshape(4, 128, 384)

    def widen(k):
        if k == 0:
            for m in range(3):
                wz_wait(m, 4)
        for m, block_q in enumerate((ql, qr, qo)):
            wd[m, k] = weights(block_q, k)

    def cg_add(k):
        g_core_wait(1, k)
        rows = slice(k % 2 * 64, k % 2 * 64 + 64)
        total = acc[:, rows]
        for m, slot in enumerate((0, 3, 1 if k < 4 else 2)):
            part = gb[1, k // 2, slot, :, rows].reshape(256, 384)
            total = total + dot_nt(part, wd[m, k // 2]).reshape(4, 64, 384)
        acc[:, rows] = total

    def cg_store():
        back = one_hot(384, 384, lambda r, c: c == 4 * (r % 96) + r // 96)
        cg_ref[...] = dot_nn(acc[...].reshape(512, 384).astype(BF), back).astype(BF)

    g_twin_send(0, 0)
    g_own(0, 0)
    g_twin_send(0, 1)
    g_own(0, 1)
    g_twin_send(0, 2)
    g_own(0, 2)
    g_twin_send(0, 3)
    g_own(0, 3)
    g_twin_send(0, 4)
    g_twin_send(0, 5)
    g_twin_send(0, 7)
    prep()
    wy_own()
    g_fwd_own(0, 0)
    g_own(0, 4)
    g_twin(0, 0)
    g_fwd_own(0, 1)
    g_own(0, 5)
    g_twin(0, 1)
    g_fwd_own(0, 2)
    g_own(0, 6)
    g_twin(0, 2)
    g_twin_send(0, 6)
    g_fwd_own(0, 3)
    g_own(0, 7)
    g_twin(0, 3)
    c_own(0)
    g_core_own(0, 0)
    g_twin(0, 4)
    g_fwd_own(0, 4)
    g_fwd_twin(0, 0)
    g_twin(0, 5)
    g_twin(0, 7)
    g_core_own(0, 1)
    g_fwd_twin(0, 1)
    g_fwd_own(0, 5)
    g_fwd_twin(0, 2)
    g_core_own(0, 2)
    g_fwd_own(0, 6)
    wy_fwd(0)
    wz_step(0, 1)
    wy_fwd(1)
    wz_step(1, 1)
    g_fwd_twin(0, 3)
    g_fwd_twin(0, 4)
    g_twin(0, 6)
    c_own(1)
    g_core_own(0, 3)
    g_core_twin(0, 0)
    g_fwd_own(0, 7)
    g_fwd_twin(0, 5)
    c_own(2)
    c_fwd(0, 0)
    c_fwd(1, 0)
    g_fwd_twin(0, 7)
    wz_step(0, 2)
    g_core_twin(0, 1)
    g_core_own(0, 4)
    g_core_twin(0, 2)
    wz_step(1, 2)
    g_core_twin(0, 3)
    g_core_twin(0, 4)
    wz_step(2, 1)
    g_core_own(0, 5)
    wz_step(0, 3)
    g_fwd_twin(0, 6)
    g_core_own(0, 6)
    g_core_twin(0, 5)
    g_core_twin(0, 7)
    c_fwd(0, 1)
    wz_step(1, 3)
    c_fwd(1, 1)
    t_send(1)
    g_core_own(0, 7)
    g_core_twin(0, 6)
    wz_step(2, 2)
    cg_own()
    wz_step(0, 4)
    c_fwd(0, 2)
    c_fwd(1, 2)
    t_send(0)
    t_send(2)
    t_send(3)
    t_send(5)
    t_send(6)
    wz_step(1, 4)
    t_send(4)
    t_send(7)
    wz_step(2, 3)
    kg_part(0)
    kg_part(1)
    wz_step(2, 4)
    t_wait(1)
    g_twin_send(1, 1)
    g_own(1, 1)
    rs_step(0, 1)
    kg_part(2)
    t_wait(0)
    g_twin_send(1, 0)
    g_own(1, 0)
    rs_step(1, 1)
    t_wait(2)
    g_twin_send(1, 2)
    g_own(1, 2)
    g_fwd_own(1, 1)
    widen(0)
    t_wait(3)
    g_twin_send(1, 3)
    g_own(1, 3)
    rs_step(0, 2)
    t_wait(5)
    g_twin_send(1, 5)
    g_own(1, 5)
    t_wait(6)
    g_twin_send(1, 6)
    g_own(1, 6)
    widen(1)
    rs_step(2, 1)
    t_wait(4)
    g_twin_send(1, 4)
    g_own(1, 4)
    t_wait(7)
    g_twin_send(1, 7)
    rs_step(1, 2)
    g_own(1, 7)
    g_fwd_own(1, 0)
    g_twin(1, 1)
    g_core_own(1, 1)
    g_fwd_own(1, 2)
    widen(2)
    rs_step(0, 3)
    g_twin(1, 0)
    g_twin(1, 2)
    g_fwd_own(1, 3)
    g_fwd_own(1, 5)
    widen(3)
    rs_step(2, 2)
    g_twin(1, 3)
    g_fwd_own(1, 4)
    rs_step(1, 3)
    g_twin(1, 5)
    g_fwd_own(1, 6)
    g_twin(1, 6)
    g_fwd_own(1, 7)
    rs_finish(0)
    g_fwd_twin(1, 1)
    g_core_own(1, 0)
    g_twin(1, 4)
    g_fwd_twin(1, 0)
    g_twin(1, 7)
    g_fwd_twin(1, 2)
    rs_step(2, 3)
    g_core_own(1, 2)
    g_fwd_twin(1, 3)
    rs_finish(1)
    g_fwd_twin(1, 5)
    g_fwd_twin(1, 6)
    g_core_own(1, 3)
    g_core_twin(1, 1)
    g_core_own(1, 5)
    g_fwd_twin(1, 4)
    g_core_twin(1, 0)
    cg_add(1)
    g_core_own(1, 4)
    g_fwd_twin(1, 7)
    rs_finish(2)
    g_core_twin(1, 2)
    cg_add(0)
    g_core_own(1, 6)
    g_core_twin(1, 3)
    g_core_twin(1, 5)
    cg_add(2)
    g_core_own(1, 7)
    g_core_twin(1, 6)
    cg_add(3)
    g_core_twin(1, 4)
    cg_add(5)
    g_core_twin(1, 7)
    cg_add(6)
    cg_add(4)
    cg_add(7)
    kg_store()
    cg_store()
    for wait in sends:
        wait()


def local(context, out_grad, kept_values, keep_codes):
    dma = pltpu.SemaphoreType.DMA
    return pl.pallas_call(
        kernel,
        out_shape=(
            jax.ShapeDtypeStruct((512, 384), BF),
            jax.ShapeDtypeStruct((192, 1536), BF),
        ),
        in_specs=[pl.BlockSpec(memory_space=pl.ANY)] * 4,
        out_specs=(pl.BlockSpec(memory_space=pltpu.VMEM),) * 2,
        scratch_shapes=[
            pltpu.VMEM((2, 4, 4, 4, 128, 384), BF),
            pltpu.VMEM((4, 3, 512, 128), BF),
            pltpu.VMEM((128, 2048), BF),
            pltpu.VMEM((4, 8, 144, 384), BF),
            pltpu.VMEM((192, 1536), BF),
            pltpu.VMEM((96, 1536), jnp.int32),
            pltpu.VMEM((3, 8, 8, 1536), F32),
            pltpu.VMEM((3, 7, 8, 1536), F32),
            pltpu.VMEM((3, 8, 16, 768), BF),
            pltpu.VMEM((4, 128, 384), F32),
            pltpu.VMEM((3, 4, 384, 384), BF),
            dma((9,)),

            dma((16, 9)),
            dma((16, 9)),
            dma((8,)),
            dma((8,)),
            dma((3, 6)),
            dma((3, 6)),
            dma((3,)),
            dma((3,)),
            dma((3, 7)),
            dma((3, 7)),
            dma((3, 7)),
            dma((3, 7)),
            dma((3, 7)),
            dma((3, 7)),
        ],
        compiler_params=pltpu.CompilerParams(
            collective_id=0, has_side_effects=True, vmem_limit_bytes=56 << 20
        ),
        cost_estimate=pl.CostEstimate(
            flops=4 * 2048 * 384 * 1536, bytes_accessed=3 << 20, transcendentals=0
        ),
        name="sparse_backward",
    )(context, out_grad, kept_values, keep_codes)

def solution(mesh):
    in_specs = (
        P(("rep", "gx"), ("gy", "gz")),
        P(("rep", "gy", "gz"), "gx"),
        P(("gy", "gz"), "gx"),
        P(("gy", "gz"), "gx"),
    )
    out_specs = (P(("rep", "gx"), ("gy", "gz")), P(("gy", "gz"), "gx"))
    return jax.shard_map(local, mesh=mesh, in_specs=in_specs, out_specs=out_specs, check_vma=False)
```

```python
import jax
import jax.numpy as jnp
from jax import lax
from jax.experimental import pallas as pl
from jax.experimental.pallas import tpu as pltpu
from jax.sharding import PartitionSpec as P

MESH = pl.DeviceIdType.MESH
BF = jnp.bfloat16
F32 = jnp.float32

def dot_nn(a, b):
    return lax.dot_general(a, b, (((1,), (0,)), ((), ())), preferred_element_type=F32)

def dot_nt(a, b):
    return lax.dot_general(a, b, (((1,), (1,)), ((), ())), preferred_element_type=F32)

def one_hot(rows, cols, hit):
    r = lax.broadcasted_iota(jnp.int32, (rows, cols), 0)
    c = lax.broadcasted_iota(jnp.int32, (rows, cols), 1)
    return jnp.where(hit(r, c), 1.0, 0.0).astype(BF)

def kernel(
    ctx_hbm, grad_hbm, kept_hbm, codes_hbm, cg_hbm, kg_hbm, cg_ref, kg_ref,
    gb, cb, cpt, ws, kept_v, codes_v, rs_out, rs_in, ag, acc, wd,
    load_sem, gs, gr, ts, tr, cs, cr, wys, wyr, wzs, wzr, rss, rsr, ags, agr,
):
    z = lax.axis_index("rep")
    q = lax.axis_index("gx")
    p = lax.axis_index("gy")
    x = lax.axis_index("gz")
    core = p % 2
    twin_p = (p + 2) % 4
    core_p = p + 1 - 2 * core
    core_twin_p = (core_p + 2) % 4
    xr, xl = (x + 1) % 4, (x + 3) % 4
    qr, ql, qo = (q + 1) % 4, (q + 3) % 4, (q + 2) % 4
    up = 1 - 2 * core

    at_twin = (z, q, twin_p, x)
    at_core = (z, q, core_p, x)
    at_xr = (z, q, p, xr)
    at_xl = (z, q, p, xl)
    at_qr = (z, qr, p, x)
    at_ql = (z, ql, p, x)
    delta = (p - q + 4) % 4
    t_slots = ((delta * delta - delta) // 2, (delta // 2) * delta)
    at_source = (z, (q + 3 - (p + 1) // 2) % 4, q, x)

    def at_z(step):
        return ((z + step + 8) % 8, q, p, x)

    sends = []

    def copy(src, dst, ssem, rsem, device):
        return pltpu.make_async_remote_copy(
            src_ref=src, dst_ref=dst, send_sem=ssem, recv_sem=rsem,
            device_id=device, device_id_type=MESH,
        )

    loads = []
    for k in range(4):
        loads.append(pltpu.make_async_copy(
            grad_hbm.at[:, pl.ds(k * 384, 384)], gb.at[0, k, p, x], load_sem.at[k]))
    for j in range(3):
        loads.append(pltpu.make_async_copy(
            ctx_hbm.at[:, pl.ds(j * 128, 128)], cb.at[q, j], load_sem.at[4 + j]))
    loads.append(pltpu.make_async_copy(kept_hbm, kept_v, load_sem.at[7]))
    loads.append(pltpu.make_async_copy(codes_hbm, codes_v, load_sem.at[8]))
    for ld in loads:
        ld.start()

    barrier = pltpu.get_barrier_semaphore()
    for device in [at_twin, at_core, at_xr, at_xl, at_qr, at_ql] + [at_z(s) for s in range(1, 8)]:
        pl.semaphore_signal(barrier, inc=1, device_id=device, device_id_type=MESH)

    pl.semaphore_signal(barrier, inc=1, device_id=at_source, device_id_type=MESH)

    @pl.when(delta != 0)
    def _():
        pl.semaphore_signal(
            barrier, inc=1, device_id=(z, p, t_slots[0], x), device_id_type=MESH)

    @pl.when(delta == 2)
    def _():
        pl.semaphore_signal(
            barrier, inc=1, device_id=(z, p, t_slots[1], x), device_id_type=MESH)

    for ld in loads[:4]:
        ld.wait()
    pl.semaphore_wait(barrier, jnp.where(delta == 0, 14, jnp.where(delta == 2, 16, 15)))

    def prep():
        loads[7].wait()
        loads[8].wait()
        split = one_hot(192, 192, lambda r, c: c == 2 * (r % 96) + r // 96)
        for k in range(4):
            cols = pl.ds(k * 384, 384)
            both = dot_nn(split, kept_v[:, cols]).astype(BF)
            numbers = codes_v[:, cols].astype(F32).astype(BF)
            ws[q, k] = both[:144]
            ws[q, 4 + k, 0:48] = both[144:]
            ws[q, 4 + k, 48:144] = numbers

    def guarded(ph, k, block_p, run):
        if ph == 0:
            run()
        else:
            pl.when(block_p != (2 if k < 4 else 1))(run)

    def g_copy(ph, k, block, si, ri, device):
        ref = gb.at[ph, k // 2, block[0], block[1], pl.ds(k % 2 * 64, 64)]
        return copy(ref, ref, gs.at[ph * 8 + k, si], gr.at[ph * 8 + k, ri], device)

    def g_send(ph, k, block, si, ri, device):
        guarded(ph, k, block[0], lambda: g_copy(ph, k, block, si, ri, device).start())
        sends.append(lambda: guarded(
            ph, k, block[0], lambda: g_copy(ph, k, block, si, ri, device).wait_send()))

    def g_wait(ph, k, block, ri):
        guarded(ph, k, block[0], lambda: g_copy(ph, k, block, 0, ri, at_core).wait_recv())

    def g_row(ph, k, block_p, si, ri):
        ref = gb.at[ph, k // 2, block_p, pl.ds(0, 4), pl.ds(k % 2 * 64, 64)]
        return copy(ref, ref, gs.at[ph * 8 + k, si], gr.at[ph * 8 + k, ri], at_core)

    def g_core(ph, k, block_p, si, ri):
        guarded(ph, k, block_p, lambda: g_row(ph, k, block_p, si, ri).start())
        sends.append(lambda: guarded(
            ph, k, block_p, lambda: g_row(ph, k, block_p, si, ri).wait_send()))

    def g_core_wait(ph, k):
        guarded(ph, k, core_p, lambda: g_row(ph, k, core_p, 7, 7).wait_recv())
        guarded(ph, k, core_twin_p, lambda: g_row(ph, k, core_twin_p, 8, 8).wait_recv())

    def g_twin_send(ph, k):
        g_send(ph, k, (p, x), 0, 0, at_twin)

    def g_own(ph, k):
        g_send(ph, k, (p, x), 1, 1, at_xr)
        g_send(ph, k, (p, x), 2, 2, at_xl)

    def g_twin(ph, k):
        g_wait(ph, k, (twin_p, x), 0)
        g_send(ph, k, (twin_p, x), 3, 3, at_xr)
        g_send(ph, k, (twin_p, x), 4, 4, at_xl)

    def g_fwd_own(ph, k):
        g_wait(ph, k, (p, xl), 1)
        g_send(ph, k, (p, xl), 5, 5, at_xr)

    def g_fwd_twin(ph, k):
        g_wait(ph, k, (twin_p, xr), 4)
        g_send(ph, k, (twin_p, xr), 6, 6, at_xl)

    def g_core_own(ph, k):
        g_wait(ph, k, (p, xr), 2)
        g_wait(ph, k, (p, (x + 2) % 4), 5)
        g_core(ph, k, p, 7, 7)

    def g_core_twin(ph, k):
        g_wait(ph, k, (twin_p, xl), 3)
        g_wait(ph, k, (twin_p, (x + 2) % 4), 6)
        g_core(ph, k, twin_p, 8, 8)

    def t_copy(k):
        slot, rows = t_slots[k // 4], pl.ds(k % 2 * 64, 64)
        return copy(gb.at[0, k // 2, p, x, rows], gb.at[1, k // 2, slot, x, rows],
                    ts.at[k], tr.at[k], (z, p, slot, x))

    def t_send(k):
        pl.when(delta != 0)(lambda: t_copy(k).start())
        sends.append(lambda: pl.when(delta != 0)(lambda: t_copy(k).wait_send()))

    def t_wait(k):
        ref = gb.at[1, k // 2, p, x, pl.ds(k % 2 * 64, 64)]
        guarded(1, k, p, lambda: copy(ref, ref, ts.at[k], tr.at[k], at_core).wait_recv())

    def c_copy(j, block_q, ri, device):
        ref = cb.at[block_q, j, pl.ds((0, 256, 0, 256, 256, 0)[ri], 256)]
        return copy(ref, ref, cs.at[j, ri], cr.at[j, ri], device)

    def c_send(j, block_q, ri, device):
        c_copy(j, block_q, ri, device).start()
        sends.append(lambda: c_copy(j, block_q, ri, device).wait_send())

    def c_own(j):
        loads[4 + j].wait()
        c_send(j, q, 0, at_qr)
        c_send(j, q, 1, at_ql)
        c_send(j, q, 4, at_qr)
        c_send(j, q, 5, at_ql)

    def c_fwd(way, j):
        if way == 0:
            c_copy(j, ql, 0, at_qr).wait_recv()
            c_send(j, ql, 2, at_qr)
        else:
            c_copy(j, qr, 1, at_qr).wait_recv()
            c_send(j, qr, 3, at_ql)

    def c_last(j):
        for ri, block_q in ((4, ql), (5, qr), (2, qo), (3, qo)):
            c_copy(j, block_q, ri, at_qr).wait_recv()

    def wy_copy(block_q, ri, device):
        ref = ws.at[block_q, z]
        return copy(ref, ref, wys.at[ri], wyr.at[ri], device)

    def wy_own():
        for ri, device in ((0, at_qr), (1, at_ql)):
            wy_copy(q, ri, device).start()
            sends.append(lambda ri=ri, device=device: wy_copy(q, ri, device).wait_send())

    def wy_fwd(way):
        if way == 0:
            wy_copy(ql, 0, at_qr).wait_recv()
            pl.when(core == 0)(lambda: wy_copy(ql, 2, at_qr).start())
        else:
            wy_copy(qr, 1, at_qr).wait_recv()
            pl.when(core == 1)(lambda: wy_copy(qr, 2, at_ql).start())
            sends.append(lambda: wy_copy(ql, 2, at_qr).wait_send())

    def wz_copy(m, block_q, slice_z, ri, device):
        ref = ws.at[block_q, slice_z]
        return copy(ref, ref, wzs.at[m, ri], wzr.at[m, ri], device)

    def wz_send(m, step):
        block_q = (ql, qr, qo)[m]
        todo = []
        if step <= 4:
            todo.append(((z - (step - 1) * up + 8) % 8, step - 1, at_z(up)))
        if step <= 3:
            todo.append(((z + (step - 1) * up + 8) % 8, 3 + step, at_z(-up)))
        for slice_z, ri, device in todo:
            wz_copy(m, block_q, slice_z, ri, device).start()
            sends.append(lambda a=(m, block_q, slice_z, ri, device): wz_copy(*a).wait_send())

    def wz_wait(m, step):
        block_q = (ql, qr, qo)[m]
        wz_copy(m, block_q, (z - step * up + 8) % 8, step - 1, at_core).wait_recv()
        if step <= 3:
            wz_copy(m, block_q, (z + step * up + 8) % 8, 3 + step, at_core).wait_recv()

    def wz_step(m, step):
        if step > 1:
            wz_wait(m, step - 1)
        elif m == 2:
            wy_copy(qo, 2, at_qr).wait_recv()
        wz_send(m, step)

    def kg_part(j):
        c_last(j)
        turn = one_hot(128, 128, lambda r, c: c == 4 * (r % 32) + r // 32)
        for b in range(4):
            cpt[:, b * 512:(b + 1) * 512] = dot_nt(turn, cb[b, j]).astype(BF)

        for k in range(4):
            cols = pl.ds(k * 384, 384)
            dense = dot_nn(cpt[...], gb[0, k].reshape(2048, 384))
            codes = codes_v[32 * j:32 * j + 32, cols]
            d0, d1, d2, d3 = (dense[32 * s:32 * s + 32] for s in range(4))
            first = jnp.where(codes < 3, d0, jnp.where(codes < 5, d1, d2))
            second = jnp.where(
                codes == 0, d1, jnp.where((codes == 1) | (codes == 3), d2, d3))
            for s in range(4):
                rs_out[j, s, :, cols] = first[8 * s:8 * s + 8]
                rs_out[j, 4 + s, :, cols] = second[8 * s:8 * s + 8]
        rs_send(j, 1)

    def rs_copy(j, step, way):
        if way == 0:
            ref, slot, device = rs_out.at[j, (z + (5 - step) * up + 8) % 8], step - 1, at_z(up)
        else:
            ref, slot, device = rs_out.at[j, (z - (4 - step) * up + 8) % 8], 3 + step, at_z(-up)
        return copy(ref, rs_in.at[j, slot], rss.at[j, slot], rsr.at[j, slot], device)

    def rs_send(j, step):
        for way in range(2 if step < 4 else 1):
            rs_copy(j, step, way).start()
            sends.append(lambda way=way: rs_copy(j, step, way).wait_send())

    def rs_step(j, step):
        rs_copy(j, step, 0).wait_recv()
        rs_out[j, (z + (4 - step) * up + 8) % 8] += rs_in[j, step - 1]
        rs_copy(j, step, 1).wait_recv()
        rs_out[j, (z - (3 - step) * up + 8) % 8] += rs_in[j, 3 + step]
        rs_send(j, step + 1)

    def ag_copy(j, step, slice_z):
        ref = ag.at[j, slice_z]
        return copy(ref, ref, ags.at[j, step - 1], agr.at[j, step - 1], at_z(step))

    def rs_finish(j):
        rs_copy(j, 4, 0).wait_recv()
        total = (rs_out[j, z] + rs_in[j, 3]) * (16384.0 ** -0.5)
        ag[j, z] = jnp.concatenate([total[:, :768], total[:, 768:]], 0).astype(BF)
        for step in (4, 3, 5, 2, 6, 1, 7):
            ag_copy(j, step, z).start()
            sends.append(lambda step=step: ag_copy(j, step, z).wait_send())

    def ag_wait(j):
        for step in range(1, 8):
            ag_copy(j, step, (z - step + 8) % 8).wait_recv()

    kg_out = pltpu.make_async_copy(kg_ref, kg_hbm, load_sem.at[9])
    cg_out = pltpu.make_async_copy(cg_ref, cg_hbm, load_sem.at[10])

    def kg_store():
        for j in range(3):
            ag_wait(j)
        rows = ag[...].reshape(384, 768)
        for h in range(2):
            def hit(r, c, h=h):
                slot, group = r % 2, r // 2
                want = (((group // 32) * 8 + slot * 4 + (group % 32) // 8) * 2 + h) * 8 + group % 8
                return c == want

            kg_ref[:, h * 768:(h + 1) * 768] = dot_nn(one_hot(192, 384, hit), rows).astype(BF)

    def weights(block_q, k):
        top, low = ws[block_q, k], ws[block_q, 4 + k]
        k0 = top[:96].astype(F32)
        k1 = jnp.concatenate([top[96:], low[:48]], 0).astype(F32)
        code = low[48:].astype(F32)
        w0 = jnp.where(code < 2.5, k0, 0.0)
        w1 = jnp.where(code < 0.5, k1, jnp.where((code > 2.5) & (code < 4.5), k0, 0.0))
        is2 = ((code > 0.5) & (code < 1.5)) | ((code > 2.5) & (code < 3.5))
        w2 = jnp.where(code > 4.5, k0, jnp.where(is2, k1, 0.0))
        is3 = ((code > 1.5) & (code < 2.5)) | (code > 3.5)
        w3 = jnp.where(is3, k1, 0.0)
        return jnp.concatenate([w0, w1, w2, w3], 0).astype(BF)

    def cg_own():
        for k in range(8):
            g_core_wait(0, k)
        total = jnp.zeros((512, 384), F32)
        for k in range(4):
            total = total + dot_nt(gb[0, k, q].reshape(512, 384), weights(q, k))
        acc[...] = total.reshape(4, 128, 384)

    def widen(k):
        if k == 0:
            for m in range(3):
                wz_wait(m, 4)
        for m, block_q in enumerate((ql, qr, qo)):
            wd[m, k] = weights(block_q, k)

    def cg_add(k):
        g_core_wait(1, k)
        rows = slice(k % 2 * 64, k % 2 * 64 + 64)
        total = acc[:, rows]
        for m, slot in enumerate((0, 3, 1 if k < 4 else 2)):
            part = gb[1, k // 2, slot, :, rows].reshape(256, 384)
            total = total + dot_nt(part, wd[m, k // 2]).reshape(4, 64, 384)
        acc[:, rows] = total

    def cg_store():
        back = one_hot(384, 384, lambda r, c: c == 4 * (r % 96) + r // 96)
        cg_ref[...] = dot_nn(acc[...].reshape(512, 384).astype(BF), back).astype(BF)

    g_twin_send(0, 0)
    g_own(0, 0)
    g_twin_send(0, 1)
    g_own(0, 1)
    g_twin_send(0, 2)
    g_own(0, 2)
    g_twin_send(0, 3)
    g_own(0, 3)
    g_twin_send(0, 4)
    g_twin_send(0, 5)
    g_twin_send(0, 7)
    prep()
    wy_own()
    g_fwd_own(0, 0)
    g_own(0, 4)
    g_twin(0, 0)
    g_fwd_own(0, 1)
    g_own(0, 5)
    g_twin(0, 1)
    g_fwd_own(0, 2)
    g_own(0, 6)
    g_twin(0, 2)
    g_twin_send(0, 6)
    g_fwd_own(0, 3)
    g_own(0, 7)
    g_twin(0, 3)
    c_own(0)
    g_core_own(0, 0)
    g_twin(0, 4)
    g_fwd_own(0, 4)
    g_fwd_twin(0, 0)
    g_twin(0, 5)
    g_twin(0, 7)
    g_core_own(0, 1)
    g_fwd_twin(0, 1)
    g_fwd_own(0, 5)
    g_fwd_twin(0, 2)
    g_core_own(0, 2)
    g_fwd_own(0, 6)
    wy_fwd(0)
    wz_step(0, 1)
    wy_fwd(1)
    wz_step(1, 1)
    g_fwd_twin(0, 3)
    g_fwd_twin(0, 4)
    g_twin(0, 6)
    c_own(1)
    g_core_own(0, 3)
    g_core_twin(0, 0)
    g_fwd_own(0, 7)
    g_fwd_twin(0, 5)
    c_own(2)
    c_fwd(0, 0)
    c_fwd(1, 0)
    g_fwd_twin(0, 7)
    wz_step(0, 2)
    g_core_twin(0, 1)
    g_core_own(0, 4)
    g_core_twin(0, 2)
    wz_step(1, 2)
    g_core_twin(0, 3)
    g_core_twin(0, 4)
    wz_step(2, 1)
    g_core_own(0, 5)
    wz_step(0, 3)
    g_fwd_twin(0, 6)
    g_core_own(0, 6)
    g_core_twin(0, 5)
    g_core_twin(0, 7)
    c_fwd(0, 1)
    wz_step(1, 3)
    c_fwd(1, 1)
    t_send(1)
    g_core_own(0, 7)
    g_core_twin(0, 6)
    wz_step(2, 2)
    cg_own()
    wz_step(0, 4)
    c_fwd(0, 2)
    c_fwd(1, 2)
    t_send(0)
    t_send(2)
    t_send(3)
    t_send(5)
    t_send(6)
    wz_step(1, 4)
    t_send(4)
    t_send(7)
    wz_step(2, 3)
    kg_part(0)
    kg_part(1)
    wz_step(2, 4)
    t_wait(1)
    g_twin_send(1, 1)
    g_own(1, 1)
    rs_step(0, 1)
    kg_part(2)
    t_wait(0)
    g_twin_send(1, 0)
    g_own(1, 0)
    rs_step(1, 1)
    t_wait(2)
    g_twin_send(1, 2)
    g_own(1, 2)
    g_fwd_own(1, 1)
    widen(0)
    t_wait(3)
    g_twin_send(1, 3)
    g_own(1, 3)
    rs_step(0, 2)
    t_wait(5)
    g_twin_send(1, 5)
    g_own(1, 5)
    t_wait(6)
    g_twin_send(1, 6)
    g_own(1, 6)
    widen(1)
    rs_step(2, 1)
    t_wait(4)
    g_twin_send(1, 4)
    g_own(1, 4)
    t_wait(7)
    g_twin_send(1, 7)
    rs_step(1, 2)
    g_own(1, 7)
    g_fwd_own(1, 0)
    g_twin(1, 1)
    g_core_own(1, 1)
    g_fwd_own(1, 2)
    widen(2)
    rs_step(0, 3)
    g_twin(1, 0)
    g_twin(1, 2)
    g_fwd_own(1, 3)
    g_fwd_own(1, 5)
    widen(3)
    rs_step(2, 2)
    g_twin(1, 3)
    g_fwd_own(1, 4)
    rs_step(1, 3)
    g_twin(1, 5)
    g_fwd_own(1, 6)
    g_twin(1, 6)
    g_fwd_own(1, 7)
    rs_finish(0)
    g_fwd_twin(1, 1)
    g_core_own(1, 0)
    g_twin(1, 4)
    g_fwd_twin(1, 0)
    g_twin(1, 7)
    g_fwd_twin(1, 2)
    rs_step(2, 3)
    g_core_own(1, 2)
    g_fwd_twin(1, 3)
    rs_finish(1)
    g_fwd_twin(1, 5)
    g_fwd_twin(1, 6)
    g_core_own(1, 3)
    g_core_twin(1, 1)
    g_core_own(1, 5)
    g_fwd_twin(1, 4)
    g_core_twin(1, 0)
    cg_add(1)
    g_core_own(1, 4)
    g_fwd_twin(1, 7)
    rs_finish(2)
    g_core_twin(1, 2)
    cg_add(0)
    g_core_own(1, 6)
    g_core_twin(1, 3)
    g_core_twin(1, 5)
    cg_add(2)
    g_core_own(1, 7)
    g_core_twin(1, 6)
    cg_add(3)
    g_core_twin(1, 4)
    cg_add(5)
    g_core_twin(1, 7)
    cg_add(6)
    cg_add(4)
    kg_store()
    kg_out.start()
    for wait in sends:
        wait()
    cg_add(7)
    cg_store()
    cg_out.start()
    kg_out.wait()
    cg_out.wait()


def local(context, out_grad, kept_values, keep_codes):
    dma = pltpu.SemaphoreType.DMA
    return pl.pallas_call(
        kernel,
        out_shape=(
            jax.ShapeDtypeStruct((512, 384), BF),
            jax.ShapeDtypeStruct((192, 1536), BF),
        ),
        in_specs=[pl.BlockSpec(memory_space=pl.ANY)] * 4,
        out_specs=(pl.BlockSpec(memory_space=pl.ANY),) * 2,
        scratch_shapes=[
            pltpu.VMEM((512, 384), BF),
            pltpu.VMEM((192, 1536), BF),
            pltpu.VMEM((2, 4, 4, 4, 128, 384), BF),
            pltpu.VMEM((4, 3, 512, 128), BF),
            pltpu.VMEM((128, 2048), BF),
            pltpu.VMEM((4, 8, 144, 384), BF),
            pltpu.VMEM((192, 1536), BF),
            pltpu.VMEM((96, 1536), jnp.int32),
            pltpu.VMEM((3, 8, 8, 1536), F32),
            pltpu.VMEM((3, 7, 8, 1536), F32),
            pltpu.VMEM((3, 8, 16, 768), BF),
            pltpu.VMEM((4, 128, 384), F32),
            pltpu.VMEM((3, 4, 384, 384), BF),
            dma((11,)),

            dma((16, 9)),
            dma((16, 9)),
            dma((8,)),
            dma((8,)),
            dma((3, 6)),
            dma((3, 6)),
            dma((3,)),
            dma((3,)),
            dma((3, 7)),
            dma((3, 7)),
            dma((3, 7)),
            dma((3, 7)),
            dma((3, 7)),
            dma((3, 7)),
        ],
        compiler_params=pltpu.CompilerParams(
            collective_id=0, has_side_effects=True, vmem_limit_bytes=56 << 20
        ),
        cost_estimate=pl.CostEstimate(
            flops=4 * 2048 * 384 * 1536, bytes_accessed=3 << 20, transcendentals=0
        ),
        name="sparse_backward",
    )(context, out_grad, kept_values, keep_codes)

def solution(mesh):
    in_specs = (
        P(("rep", "gx"), ("gy", "gz")),
        P(("rep", "gy", "gz"), "gx"),
        P(("gy", "gz"), "gx"),
        P(("gy", "gz"), "gx"),
    )
    out_specs = (P(("rep", "gx"), ("gy", "gz")), P(("gy", "gz"), "gx"))
    return jax.shard_map(local, mesh=mesh, in_specs=in_specs, out_specs=out_specs, check_vma=False)
```
